32 devices in a mesh: pop: 2 (over x), blk: 16 (over z, y, core).
Axes of the slice: x: 2, y: 2, z: 4, core: 2. Of those that a mesh axis runs over, the one named last changes fastest.
Arguments:
- v_init: float32 [128, 2, 16384], P('pop', None, 'blk'), may hold values from -6 to 6
- a_init: float32 [128, 2, 16384], P('pop', None, 'blk'), may hold values from 0 to 1
- z_init: bfloat16 [128, 2, 16384], P('pop', None, 'blk'), may hold values from 0 to 1
- base_weight: bfloat16 [16384, 16384], P('blk', 'pop'), may hold values from -0.046875 to 0.046875
- factor_u: bfloat16 [128, 4, 16384], P('pop', None, 'blk'), may hold values from -6 to 6
- factor_v: bfloat16 [128, 4, 16384], P('pop', None, 'blk'), may hold values from -0.046875 to 0.046875
- in_weight: bfloat16 [700, 16384], P(None, 'blk'), may hold values from -0.21875 to 0.21875
- spikes_in: int32 [2, 2, 700], replicated, may hold values 0 or 1
- step_count: int32 [128, 2], P('pop'), may hold values from 1 to 2, as said below
- member_ids: int32 [128], P('pop'), may hold values from 0 to 127, each once
- decay_mem: float32 [16384], P('blk'), may hold values from 0.3 to 0.9
- decay_adapt: float32 [16384], P('blk'), may hold values from 0.5 to 0.95
- thr_base: float32 [16384], P('blk'), may hold values from 0.2 to 1
- thr_adapt: float32 [16384], P('blk'), may hold values from 0.5 to 2
Outputs:
- v_out: float32 [128, 2, 16384], P('pop', None, 'blk')
- a_out: float32 [128, 2, 16384], P('pop', None, 'blk')
The draws below stay inside these ranges and needn't reach their ends.
Inputs may be any that keep to these rules, and one draw needn't show every extreme that they name: `member_ids`: each member appears in exactly one slot. `step_count`: a trial's state stops changing after its last step.
All inputs are finite; a program needn't handle non-finite values.
Results may differ from the reference program's by a relative error of at most 0.00088.
Values may be sent and summed in bfloat16 or wider, within the bound.
A program may use at most 128 MiB of HBM per device.

```python
import jax
import jax.numpy as jnp
from jax import lax

N = 16384
N_IN = 700
RANK = 4
STEPS = 2
TRIALS = 2
MEMBERS = 128


def draw_step_count(key, part):
    counts = jax.random.randint(key, (MEMBERS * TRIALS,), 1, STEPS + 1)
    counts = counts.at[0].set(STEPS)
    counts = counts.at[MEMBERS * TRIALS - 1].set(1)
    return counts.reshape(MEMBERS, TRIALS).astype(jnp.int32)


def place_ends(entries, stream_key, low, top_value):
    longest = entries.shape.index(max(entries.shape))
    spots = []
    for shift in (0, 1):
        where = [jax.random.randint(jax.random.fold_in(stream_key, axis), (), 0, length) for axis, length in enumerate(entries.shape)]
        where[longest] = (where[longest] + shift) % entries.shape[longest]
        spots.append(tuple(where))
    return entries.at[spots[0]].set(low).at[spots[1]].set(top_value)


def shard_levels(stream_key, shape, pieces, least, high):
    def one(axis_at, blocks):
        steps = jax.random.uniform(jax.random.fold_in(jax.random.fold_in(stream_key, 6), axis_at), (blocks,), jnp.float32, least / len(pieces), high / len(pieces))
        return jnp.repeat(jnp.exp(steps), shape[axis_at] // blocks).reshape((-1,) + (1,) * (len(shape) - axis_at - 1))

    gain = one(*pieces[0])
    for cut in pieces[1:]:
        gain = gain * one(*cut)
    return gain


def centred(rng, extent, spread, most, cuts=(), held_as=jnp.bfloat16):
    values = jax.random.normal(rng, extent, jnp.float32) * spread
    if len(cuts) > 0:
        values = shard_levels(rng, extent, cuts, -0.22, 0.18) * values
    return jnp.clip(values, min=-most, max=most).astype(held_as)


def setup_inputs(seed: int = 0) -> dict:
    arg_keys = jax.random.split(jax.random.key(seed), 15)
    v_init = centred(arg_keys[0], (MEMBERS, TRIALS, N), 1.0, 6.0, ((0, 2), (2, 16)), jnp.float32)
    a_init = jnp.clip(1.0 * jax.random.uniform(arg_keys[1], (MEMBERS, TRIALS, N), jnp.float32) ** shard_levels(arg_keys[1], (MEMBERS, TRIALS, N), ((0, 2), (2, 16)), -0.2, 0.2), 0.0, 1.0)
    z_init = jnp.clip(1.0 * jax.random.uniform(arg_keys[2], (MEMBERS, TRIALS, N), jnp.float32) ** shard_levels(arg_keys[2], (MEMBERS, TRIALS, N), ((0, 2), (2, 16)), -0.2, 0.2), 0.0, 1.0).astype(jnp.bfloat16)
    base_weight = centred(arg_keys[3], (N, N), N ** -0.5, 0.046875, ((0, 16), (1, 2)))
    factor_u = centred(arg_keys[4], (MEMBERS, RANK, N), 1.0, 6.0, ((0, 2), (2, 16)))
    factor_v = centred(arg_keys[5], (MEMBERS, RANK, N), N ** -0.5, 0.046875, ((0, 2), (2, 16)))
    in_weight = centred(arg_keys[6], (N_IN, N), N_IN ** -0.5, 0.21875, ((1, 16),))
    spikes_in = place_ends((jax.random.randint(arg_keys[7], (STEPS, TRIALS, N_IN), 0, 2) < 1).astype(jnp.int32), jax.random.fold_in(arg_keys[7], 1), 0, 1)
    step_count = draw_step_count(jax.random.fold_in(arg_keys[14], 71), 0)
    member_ids = jax.random.permutation(arg_keys[9], MEMBERS).astype(jnp.int32)
    decay_mem = jnp.clip(0.3 + 0.59999996 * jax.random.uniform(arg_keys[10], (N,), jnp.float32) ** shard_levels(arg_keys[10], (N,), ((0, 16),), -0.2, 0.2), 0.3, 0.9)
    decay_adapt = jnp.clip(0.5 + 0.45 * jax.random.uniform(arg_keys[11], (N,), jnp.float32) ** shard_levels(arg_keys[11], (N,), ((0, 16),), -0.2, 0.2), 0.5, 0.95)
    thr_base = jnp.clip(0.2 + 0.8 * jax.random.uniform(arg_keys[12], (N,), jnp.float32) ** shard_levels(arg_keys[12], (N,), ((0, 16),), -0.2, 0.2), 0.2, 1.0)
    thr_adapt = jnp.clip(0.5 + 1.5 * jax.random.uniform(arg_keys[13], (N,), jnp.float32) ** shard_levels(arg_keys[13], (N,), ((0, 16),), -0.2, 0.2), 0.5, 2.0)
    return dict(v_init=v_init, a_init=a_init, z_init=z_init, base_weight=base_weight, factor_u=factor_u, factor_v=factor_v, in_weight=in_weight, spikes_in=spikes_in, step_count=step_count, member_ids=member_ids, decay_mem=decay_mem, decay_adapt=decay_adapt, thr_base=thr_base, thr_adapt=thr_adapt)


def reference(v_init, a_init, z_init, base_weight, factor_u, factor_v, in_weight, spikes_in, step_count, member_ids, decay_mem, decay_adapt, thr_base, thr_adapt):
    sign = (1 - 2 * (member_ids % 2)).astype(jnp.float32)
    factor_uf = factor_u.astype(jnp.float32)
    factor_vf = factor_v.astype(jnp.float32)
    state_v, state_a, spikes = v_init, a_init, z_init
    for step in range(STEPS):
        spikes_f = spikes.astype(jnp.float32)
        proj = jnp.einsum("mtn,mkn->mtk", spikes_f, factor_vf).astype(jnp.bfloat16)
        low = jnp.einsum("mtk,mkn->mtn", proj.astype(jnp.float32), factor_uf)
        dense = lax.dot_general(spikes.reshape(-1, N), base_weight, (((1,), (1,)), ((), ())), preferred_element_type=jnp.float32).reshape(spikes.shape)
        current = jnp.dot(spikes_in[step].astype(jnp.bfloat16), in_weight, preferred_element_type=jnp.float32)
        drive = dense + 0.5 * sign[:, None, None] * low + current[None]
        v_new = decay_mem * state_v + (1.0 - decay_mem) * drive - spikes_f * (thr_base + thr_adapt * state_a)
        a_new = decay_adapt * state_a + (1.0 - decay_adapt) * spikes_f
        active = (step_count > step)[:, :, None]
        state_v = jnp.where(active, v_new, state_v)
        state_a = jnp.where(active, a_new, state_a)
        if step + 1 < STEPS:
            spikes = jax.nn.sigmoid(3.0 * (state_v - thr_base - thr_adapt * state_a)).astype(jnp.bfloat16)
    return state_v, state_a
```

```python
import functools

import jax
import jax.numpy as jnp
from jax import lax
from jax.experimental import pallas as pl
from jax.experimental.pallas import tpu as pltpu
from jax.sharding import PartitionSpec as P

STEPS = 2
CORES = 2
MESH = pl.DeviceIdType.MESH


def factor_plane(blks):
    chips = blks // CORES
    ys = 1
    while (2 * ys) * (2 * ys) <= chips:
        ys *= 2
    return ys, chips // ys


def kernel(
    pops, blks, halves, tiles,
    z_ref, part_ref, w_hbm, out_ref, proj_ref,
    gath, wbuf, acc, sendp, recvp, pg,
    w_sem, recv_sem, x_sem, up_sem, down_sem, y_sem, c_sem, ps_sem, pr_sem, ss_sem, sr_sem,
):
    ys, zs_all = factor_plane(blks)
    per = blks // pops
    group = ys * CORES
    srcs = per // group
    rows, block = z_ref.shape
    part = rows // halves
    outs = out_ref.shape[1]
    wide = outs // tiles

    p = lax.axis_index("pop")
    b = lax.axis_index("blk")
    c = lax.rem(b, CORES)
    y = lax.rem(b // CORES, ys)
    z = b // group
    mine = b // per
    first = p * srcs

    def at(pp, bb):
        return {"pop": pp, "blk": bb}

    def slot(i, pp, h):
        start = pl.multiple_of(pp * rows + h * part, part)
        return gath.at[i, pl.ds(start, part)]

    def index(i, pp, h):
        return (i * pops + pp) * halves + h

    def remote(src, dst, s_sem, r_sem, pp, bb):
        return pltpu.make_async_remote_copy(
            src_ref=src, dst_ref=dst, send_sem=s_sem, recv_sem=r_sem,
            device_id=at(pp, bb), device_id_type=MESH,
        )

    waits = []

    def send_if(cond, desc):
        if cond is None:
            desc.start()
        else:
            pl.when(cond)(desc.start)
        waits.append((cond, desc))

    my_i = lax.rem(b, per)
    for h in range(halves):
        src = z_ref.at[pl.ds(h * part, part)]
        r = recv_sem.at[index(my_i, p, h)]
        send_if(mine != p, remote(src, slot(my_i, p, h), x_sem.at[h], r, mine, b))

        @pl.when(mine == p)
        def _():
            pltpu.make_async_copy(src, slot(my_i, p, h), r).start()

    for d in range(1, blks):
        other = lax.rem(b + d, blks)
        send_if(None, remote(part_ref, pg.at[b], ps_sem.at[d], pr_sem.at[b], p, other))

    def w_copy(i):
        cols = pl.ds(pl.multiple_of(i * block, block), block)
        return pltpu.make_async_copy(w_hbm.at[:, cols], wbuf.at[i], w_sem.at[i])

    flip = z > first

    def source_of(g):
        return jnp.where(flip, srcs - 1 - g, g)

    for g in range(srcs):
        for j in range(group):
            w_copy(source_of(g) * group + j).start()
    acc[...] = jnp.zeros_like(acc)

    def arrive(i, pp, h):
        ref = slot(i, pp, h)
        k = index(i, pp, h)
        remote(ref, ref, x_sem.at[0], recv_sem.at[k], p, lax.rem(b + 1, blks)).wait_recv()

    def pass_on(i, pp, h, sem, cond, bb):
        k = index(i, pp, h)
        ref = slot(i, pp, h)
        send_if(cond, remote(ref, ref, sem, recv_sem.at[k], p, bb))

    def sibling():
        return (z * ys + y) * CORES + (1 - c)

    def line(g, pp, h):
        zs = source_of(g)
        i = zs * group + y * CORES + c
        k = index(i, pp, h)
        arrive(i, pp, h)
        origin = first + zs
        pass_on(i, pp, h, up_sem.at[k], (z >= origin) & (z < zs_all - 1), b + group)
        pass_on(i, pp, h, down_sem.at[k], (z <= origin) & (z > 0), b - group)
        for d in range(1, ys):
            other = (z * ys + lax.rem(y + d, ys)) * CORES + c
            pass_on(i, pp, h, y_sem.at[d, k], None, other)
        pass_on(i, pp, h, c_sem.at[k], None, sibling())

    def across(g, pp, h):
        for d in range(1, ys):
            i = source_of(g) * group + lax.rem(y + d, ys) * CORES + c
            arrive(i, pp, h)
            pass_on(i, pp, h, c_sem.at[index(i, pp, h)], None, sibling())

    def tile_dot(i, t):
        cols = pl.ds(t * wide if isinstance(t, int) else pl.multiple_of(t * wide, wide), wide)
        acc[:, cols] += lax.dot_general(
            gath[i], wbuf[i, cols, :], (((1,), (1,)), ((), ())),
            preferred_element_type=jnp.float32,
        )

    def other_core(g, yy):
        i = source_of(g) * group + yy * CORES + (1 - c)
        for q in range(pops):
            for h in range(halves):
                arrive(i, q, h)

    def ready(g):
        jobs = []
        for d in range(ys):
            yy = lax.rem(y + d, ys)
            jobs.append((source_of(g) * group + yy * CORES + c, None))
            jobs.append((source_of(g) * group + yy * CORES + (1 - c), yy))
        return [(g, i, yy) for i, yy in jobs]

    def multiply(job):
        g, i, yy = job
        if yy is not None:
            other_core(g, yy)
        w_copy(i).wait()

        @pl.loop(0, tiles)
        def _(t):
            tile_dot(i, t)

    steps = [(g, e, h) for g in range(srcs) for e in range(pops) for h in range(halves)]
    queue = []
    last = None
    for n, (g, e, h) in enumerate(steps):
        line(g, lax.rem(p + e, pops), h)
        if last is not None:
            across(last[0], lax.rem(p + last[1], pops), last[2])
            if last[0] != g:
                queue.extend(ready(last[0]))
        last = (g, e, h)
        if queue:
            multiply(queue.pop(0))
    across(last[0], lax.rem(p + last[1], pops), last[2])
    for job in queue:
        multiply(job)

    final = ready(srcs - 1)
    for g, i, yy in final:
        if yy is not None:
            other_core(g, yy)
        w_copy(i).wait()
    for t in range(tiles):
        for g, i, yy in final:
            tile_dot(i, t)
        for d in range(1, pops):
            pp = lax.rem(p + d, pops)
            half = acc[pl.ds(pl.multiple_of(pp * rows, rows), rows), pl.ds(t * wide, wide)]
            sendp[t, d] = half.astype(sendp.dtype)
            send_if(None, remote(
                sendp.at[t, d], recvp.at[t, p], ss_sem.at[t, d], sr_sem.at[t, p], pp, b))

    pg[b] = part_ref[...]
    for d in range(1, blks):
        other = lax.rem(b + d, blks)
        remote(part_ref, pg.at[other], ps_sem.at[d], pr_sem.at[other], p, other).wait_recv()
    total = pg[0]
    for d in range(1, blks):
        total = total + pg[d]
    proj_ref[...] = total

    for t in range(tiles):
        cols = pl.ds(t * wide, wide)
        value = acc[pl.ds(pl.multiple_of(p * rows, rows), rows), cols]
        for d in range(1, pops):
            pp = lax.rem(p + d, pops)
            remote(
                sendp.at[t, d], recvp.at[t, pp], ss_sem.at[t, d], sr_sem.at[t, pp], pp, b
            ).wait_recv()
            value = value + recvp[t, pp].astype(jnp.float32)
        out_ref[:, cols] = value

    for cond, desc in waits:
        if cond is None:
            desc.wait_send()
        else:
            pl.when(cond)(desc.wait_send)


def exchange(pops, blks, spikes, part, weight):
    rows, block = spikes.shape
    outs = weight.shape[0]
    per = blks // pops
    ys, _ = factor_plane(blks)
    halves = 2
    tiles = max(1, outs // 256)
    slots = blks * halves
    dma = pltpu.SemaphoreType.DMA
    vmem = pl.BlockSpec(memory_space=pltpu.VMEM)
    flops = 2 * pops * rows * weight.size
    return pl.pallas_call(
        functools.partial(kernel, pops, blks, halves, tiles),
        out_shape=(
            jax.ShapeDtypeStruct((rows, outs), jnp.float32),
            jax.ShapeDtypeStruct(part.shape, jnp.float32),
        ),
        in_specs=[vmem, vmem, pl.BlockSpec(memory_space=pl.ANY)],
        out_specs=(vmem, vmem),
        scratch_shapes=[
            pltpu.VMEM((per, pops * rows, block), spikes.dtype),
            pltpu.VMEM((per, outs, block), weight.dtype),
            pltpu.VMEM((pops * rows, outs), jnp.float32),
            pltpu.VMEM((tiles, pops, rows, outs // tiles), jnp.bfloat16),
            pltpu.VMEM((tiles, pops, rows, outs // tiles), jnp.bfloat16),
            pltpu.VMEM((blks,) + part.shape, jnp.float32),
            dma((per,)),
            dma((slots,)),
            dma((halves,)),
            dma((slots,)),
            dma((slots,)),
            dma((ys, slots)),
            dma((slots,)),
            dma((blks,)),
            dma((blks,)),
            dma((tiles, pops)),
            dma((tiles, pops)),
        ],
        compiler_params=pltpu.CompilerParams(
            has_side_effects=True, vmem_limit_bytes=40 * 2**20
        ),
        cost_estimate=pl.CostEstimate(
            flops=flops, bytes_accessed=weight.size * 2, transcendentals=0
        ),
    )(spikes, part, weight)


def body(
    pops,
    blks,
    v_init,
    a_init,
    z_init,
    base_weight,
    factor_u,
    factor_v,
    in_weight,
    spikes_in,
    step_count,
    member_ids,
    decay_mem,
    decay_adapt,
    thr_base,
    thr_adapt,
):
    members, trials, block = v_init.shape
    rank = factor_v.shape[1]
    rows = members * trials
    sign = (1 - 2 * (member_ids % 2)).astype(jnp.float32)
    state_v, state_a, spikes = (v_init, a_init, z_init)
    pad = -members % 128
    for step in range(STEPS):
        spikes_f = spikes.astype(jnp.float32)
        part = jnp.einsum(
            "mtn,mkn->tkm", spikes, factor_v, preferred_element_type=jnp.float32
        ).reshape(trials * rank, members)
        part = jnp.pad(part, ((0, 0), (0, pad)))
        dense, total = exchange(pops, blks, spikes.reshape(rows, block), part, base_weight)
        dense = dense.reshape(members, trials, block)
        proj = total[:, :members].reshape(trials, rank, members).astype(jnp.bfloat16)
        low = jnp.einsum("tkm,mkn->mtn", proj, factor_u, preferred_element_type=jnp.float32)
        current = jnp.dot(
            spikes_in[step].astype(jnp.bfloat16), in_weight, preferred_element_type=jnp.float32
        )
        drive = dense + 0.5 * sign[:, None, None] * low + current[None]
        v_new = (
            decay_mem * state_v
            + (1.0 - decay_mem) * drive
            - spikes_f * (thr_base + thr_adapt * state_a)
        )
        a_new = decay_adapt * state_a + (1.0 - decay_adapt) * spikes_f
        active = (step_count > step)[:, :, None]
        state_v = jnp.where(active, v_new, state_v)
        state_a = jnp.where(active, a_new, state_a)
        if step + 1 < STEPS:
            spikes = jax.nn.sigmoid(3.0 * (state_v - thr_base - thr_adapt * state_a)).astype(
                jnp.bfloat16
            )
    return (state_v, state_a)


def solution(mesh):
    in_specs = (
        P("pop", None, "blk"),
        P("pop", None, "blk"),
        P("pop", None, "blk"),
        P("blk", "pop"),
        P("pop", None, "blk"),
        P("pop", None, "blk"),
        P(None, "blk"),
        P(),
        P("pop", None),
        P("pop"),
        P("blk"),
        P("blk"),
        P("blk"),
        P("blk"),
    )
    out_specs = (P("pop", None, "blk"), P("pop", None, "blk"))
    return jax.shard_map(
        functools.partial(body, mesh.shape["pop"], mesh.shape["blk"]),
        mesh=mesh, in_specs=in_specs, out_specs=out_specs, check_vma=False,
    )
```

```python
import functools

import jax
import jax.numpy as jnp
from jax import lax
from jax.experimental import pallas as pl
from jax.experimental.pallas import tpu as pltpu
from jax.sharding import PartitionSpec as P

STEPS = 2
CORES = 2
MESH = pl.DeviceIdType.MESH


def factor_plane(blks):
    chips = blks // CORES
    ys = 1
    while (2 * ys) * (2 * ys) <= chips:
        ys *= 2
    return ys, chips // ys


def kernel(
    pops, blks, halves, tiles,
    z_ref, part_ref, w_hbm, out_ref, proj_ref,
    gath, wbuf, acc, sendp, recvp, pg,
    w_sem, recv_sem, x_sem, up_sem, down_sem, y_sem, c_sem, ps_sem, pr_sem, ss_sem, sr_sem,
):
    ys, zs_all = factor_plane(blks)
    per = blks // pops
    group = ys * CORES
    srcs = per // group
    rows, block = z_ref.shape
    part = rows // halves
    outs = out_ref.shape[1]
    wide = outs // tiles

    p = lax.axis_index("pop")
    b = lax.axis_index("blk")
    c = lax.rem(b, CORES)
    y = lax.rem(b // CORES, ys)
    z = b // group
    mine = b // per
    first = p * srcs

    def at(pp, bb):
        return {"pop": pp, "blk": bb}

    def slot(i, pp, h):
        start = pl.multiple_of(pp * rows + h * part, part)
        return gath.at[i, pl.ds(start, part)]

    def index(i, pp, h):
        return (i * pops + pp) * halves + h

    def remote(src, dst, s_sem, r_sem, pp, bb):
        return pltpu.make_async_remote_copy(
            src_ref=src, dst_ref=dst, send_sem=s_sem, recv_sem=r_sem,
            device_id=at(pp, bb), device_id_type=MESH,
        )

    waits = []

    def send_if(cond, desc):
        if cond is None:
            desc.start()
        else:
            pl.when(cond)(desc.start)
        waits.append((cond, desc))

    my_i = lax.rem(b, per)
    for h in range(halves):
        src = z_ref.at[pl.ds(h * part, part)]
        r = recv_sem.at[index(my_i, p, h)]
        send_if(mine != p, remote(src, slot(my_i, p, h), x_sem.at[h], r, mine, b))

        @pl.when(mine == p)
        def _():
            pltpu.make_async_copy(src, slot(my_i, p, h), r).start()

    for d in range(1, blks):
        other = lax.rem(b + d, blks)
        send_if(None, remote(part_ref, pg.at[b], ps_sem.at[d], pr_sem.at[b], p, other))

    def w_copy(i):
        cols = pl.ds(pl.multiple_of(i * block, block), block)
        return pltpu.make_async_copy(w_hbm.at[:, cols], wbuf.at[i], w_sem.at[i])

    flip = z > first

    def source_of(g):
        return jnp.where(flip, srcs - 1 - g, g)

    for g in range(srcs):
        for j in range(group):
            w_copy(source_of(g) * group + j).start()
    acc[...] = jnp.zeros_like(acc)

    def arrive(i, pp, h):
        ref = slot(i, pp, h)
        k = index(i, pp, h)
        remote(ref, ref, x_sem.at[0], recv_sem.at[k], p, lax.rem(b + 1, blks)).wait_recv()

    def pass_on(i, pp, h, sem, cond, bb):
        k = index(i, pp, h)
        ref = slot(i, pp, h)
        send_if(cond, remote(ref, ref, sem, recv_sem.at[k], p, bb))

    def sibling():
        return (z * ys + y) * CORES + (1 - c)

    def line(g, pp, h):
        zs = source_of(g)
        i = zs * group + y * CORES + c
        k = index(i, pp, h)
        arrive(i, pp, h)
        origin = first + zs
        pass_on(i, pp, h, up_sem.at[k], (z >= origin) & (z < zs_all - 1), b + group)
        pass_on(i, pp, h, down_sem.at[k], (z <= origin) & (z > 0), b - group)
        for d in range(1, ys):
            other = (z * ys + lax.rem(y + d, ys)) * CORES + c
            pass_on(i, pp, h, y_sem.at[d, k], None, other)
        pass_on(i, pp, h, c_sem.at[k], None, sibling())

    def across(g, pp, h):
        for d in range(1, ys):
            i = source_of(g) * group + lax.rem(y + d, ys) * CORES + c
            arrive(i, pp, h)
            pass_on(i, pp, h, c_sem.at[index(i, pp, h)], None, sibling())

    def tile_dot(i, t):
        cols = pl.ds(t * wide if isinstance(t, int) else pl.multiple_of(t * wide, wide), wide)
        acc[:, cols] += lax.dot_general(
            gath[i], wbuf[i, cols, :], (((1,), (1,)), ((), ())),
            preferred_element_type=jnp.float32,
        )

    def other_core(g, yy):
        i = source_of(g) * group + yy * CORES + (1 - c)
        for q in range(pops):
            for h in range(halves):
                arrive(i, q, h)

    def ready(g):
        jobs = []
        for d in range(ys):
            yy = lax.rem(y + d, ys)
            jobs.append((source_of(g) * group + yy * CORES + c, None))
            jobs.append((source_of(g) * group + yy * CORES + (1 - c), yy))
        return [(g, i, yy) for i, yy in jobs]

    def multiply(job):
        g, i, yy = job
        if yy is not None:
            other_core(g, yy)
        w_copy(i).wait()

        @pl.loop(0, tiles)
        def _(t):
            tile_dot(i, t)

    steps = [(g, e, h) for g in range(srcs) for e in range(pops) for h in range(halves)]
    queue = []
    last = None
    for n, (g, e, h) in enumerate(steps):
        line(g, lax.rem(p + e, pops), h)
        if last is not None:
            across(last[0], lax.rem(p + last[1], pops), last[2])
            if last[0] != g:
                queue.extend(ready(last[0]))
        last = (g, e, h)
        if queue:
            multiply(queue.pop(0))
    across(last[0], lax.rem(p + last[1], pops), last[2])
    for job in queue:
        multiply(job)

    final = ready(srcs - 1)
    for g, i, yy in final:
        if yy is not None:
            other_core(g, yy)
        w_copy(i).wait()
    for t in range(tiles):
        for g, i, yy in final:
            tile_dot(i, t)
        for d in range(1, pops):
            pp = lax.rem(p + d, pops)
            half = acc[pl.ds(pl.multiple_of(pp * rows, rows), rows), pl.ds(t * wide, wide)]
            sendp[t, d] = half.astype(sendp.dtype)
            send_if(None, remote(
                sendp.at[t, d], recvp.at[t, p], ss_sem.at[t, d], sr_sem.at[t, p], pp, b))

    pg[b] = part_ref[...]
    for d in range(1, blks):
        other = lax.rem(b + d, blks)
        remote(part_ref, pg.at[other], ps_sem.at[d], pr_sem.at[other], p, other).wait_recv()
    total = pg[0]
    for d in range(1, blks):
        total = total + pg[d]
    proj_ref[...] = total

    for t in range(tiles):
        cols = pl.ds(t * wide, wide)
        value = acc[pl.ds(pl.multiple_of(p * rows, rows), rows), cols]
        for d in range(1, pops):
            pp = lax.rem(p + d, pops)
            remote(
                sendp.at[t, d], recvp.at[t, pp], ss_sem.at[t, d], sr_sem.at[t, pp], pp, b
            ).wait_recv()
            value = value + recvp[t, pp].astype(jnp.float32)
        out_ref[:, cols] = value

    for cond, desc in waits:
        if cond is None:
            desc.wait_send()
        else:
            pl.when(cond)(desc.wait_send)


def exchange(pops, blks, spikes, part, weight):
    rows, block = spikes.shape
    outs = weight.shape[0]
    per = blks // pops
    ys, _ = factor_plane(blks)
    halves = 2
    tiles = max(1, outs // 256)
    slots = blks * halves
    dma = pltpu.SemaphoreType.DMA
    vmem = pl.BlockSpec(memory_space=pltpu.VMEM)
    flops = 2 * pops * rows * weight.size
    return pl.pallas_call(
        functools.partial(kernel, pops, blks, halves, tiles),
        out_shape=(
            jax.ShapeDtypeStruct((rows, outs), jnp.float32),
            jax.ShapeDtypeStruct(part.shape, jnp.float32),
        ),
        in_specs=[vmem, vmem, pl.BlockSpec(memory_space=pl.ANY)],
        out_specs=(vmem, vmem),
        scratch_shapes=[
            pltpu.VMEM((per, pops * rows, block), spikes.dtype),
            pltpu.VMEM((per, outs, block), weight.dtype),
            pltpu.VMEM((pops * rows, outs), jnp.float32),
            pltpu.VMEM((tiles, pops, rows, outs // tiles), jnp.bfloat16),
            pltpu.VMEM((tiles, pops, rows, outs // tiles), jnp.bfloat16),
            pltpu.VMEM((blks,) + part.shape, jnp.float32),
            dma((per,)),
            dma((slots,)),
            dma((halves,)),
            dma((slots,)),
            dma((slots,)),
            dma((ys, slots)),
            dma((slots,)),
            dma((blks,)),
            dma((blks,)),
            dma((tiles, pops)),
            dma((tiles, pops)),
        ],
        compiler_params=pltpu.CompilerParams(
            has_side_effects=True, vmem_limit_bytes=40 * 2**20
        ),
        cost_estimate=pl.CostEstimate(
            flops=flops, bytes_accessed=weight.size * 2, transcendentals=0
        ),
    )(spikes, part, weight)


def body(
    pops,
    blks,
    v_init,
    a_init,
    z_init,
    base_weight,
    factor_u,
    factor_v,
    in_weight,
    spikes_in,
    step_count,
    member_ids,
    decay_mem,
    decay_adapt,
    thr_base,
    thr_adapt,
):
    members, trials, block = v_init.shape
    rank = factor_v.shape[1]
    rows = members * trials
    sign = (1 - 2 * (member_ids % 2)).astype(jnp.float32)
    turn = lambda x: x.transpose(1, 0, 2)
    state_v, state_a, spikes = (turn(v_init), turn(a_init), turn(z_init))
    pad = -members % 128
    for step in range(STEPS):
        spikes_f = spikes.astype(jnp.float32)
        part = jnp.einsum(
            "tmn,mkn->tkm", spikes, factor_v, preferred_element_type=jnp.float32
        ).reshape(trials * rank, members)
        part = jnp.pad(part, ((0, 0), (0, pad)))
        dense, total = exchange(pops, blks, spikes.reshape(rows, block), part, base_weight)
        dense = dense.reshape(trials, members, block)
        proj = total[:, :members].reshape(trials, rank, members).astype(jnp.bfloat16)
        low = jnp.einsum("tkm,mkn->tmn", proj, factor_u, preferred_element_type=jnp.float32)
        current = jnp.dot(
            spikes_in[step].astype(jnp.bfloat16), in_weight, preferred_element_type=jnp.float32
        )
        drive = dense + 0.5 * sign[None, :, None] * low + current[:, None]
        v_new = (
            decay_mem * state_v
            + (1.0 - decay_mem) * drive
            - spikes_f * (thr_base + thr_adapt * state_a)
        )
        a_new = decay_adapt * state_a + (1.0 - decay_adapt) * spikes_f
        active = (step_count > step).T[:, :, None]
        state_v = jnp.where(active, v_new, state_v)
        state_a = jnp.where(active, a_new, state_a)
        if step + 1 < STEPS:
            spikes = jax.nn.sigmoid(3.0 * (state_v - thr_base - thr_adapt * state_a)).astype(
                jnp.bfloat16
            )
    return (turn(state_v), turn(state_a))


def solution(mesh):
    in_specs = (
        P("pop", None, "blk"),
        P("pop", None, "blk"),
        P("pop", None, "blk"),
        P("blk", "pop"),
        P("pop", None, "blk"),
        P("pop", None, "blk"),
        P(None, "blk"),
        P(),
        P("pop", None),
        P("pop"),
        P("blk"),
        P("blk"),
        P("blk"),
        P("blk"),
    )
    out_specs = (P("pop", None, "blk"), P("pop", None, "blk"))
    return jax.shard_map(
        functools.partial(body, mesh.shape["pop"], mesh.shape["blk"]),
        mesh=mesh, in_specs=in_specs, out_specs=out_specs, check_vma=False,
    )
```

```python
import functools

import jax
import jax.numpy as jnp
from jax import lax
from jax.experimental import pallas as pl
from jax.experimental.pallas import tpu as pltpu
from jax.sharding import PartitionSpec as P

STEPS = 2
CORES = 2
MESH = pl.DeviceIdType.MESH


def factor_plane(blks):
    chips = blks // CORES
    ys = 1
    while (2 * ys) * (2 * ys) <= chips:
        ys *= 2
    return ys, chips // ys


def kernel(
    pops, blks, halves, tiles,
    z_ref, part_ref, w_hbm, out_ref, proj_ref,
    gath, wbuf, acc, sendp, recvp, pg,
    w_sem, recv_sem, x_sem, up_sem, down_sem, y_sem, c_sem, ps_sem, pr_sem, ss_sem, sr_sem,
):
    ys, zs_all = factor_plane(blks)
    per = blks // pops
    group = ys * CORES
    srcs = per // group
    rows, block = z_ref.shape
    part = rows // halves
    outs = out_ref.shape[1]
    wide = outs // tiles

    p = lax.axis_index("pop")
    b = lax.axis_index("blk")
    c = lax.rem(b, CORES)
    y = lax.rem(b // CORES, ys)
    z = b // group
    mine = b // per
    first = p * srcs

    def at(pp, bb):
        return {"pop": pp, "blk": bb}

    def slot(i, pp, h):
        start = pl.multiple_of(pp * rows + h * part, part)
        return gath.at[i, pl.ds(start, part)]

    def index(i, pp, h):
        return (i * pops + pp) * halves + h

    def remote(src, dst, s_sem, r_sem, pp, bb):
        return pltpu.make_async_remote_copy(
            src_ref=src, dst_ref=dst, send_sem=s_sem, recv_sem=r_sem,
            device_id=at(pp, bb), device_id_type=MESH,
        )

    waits = []

    def send_if(cond, desc):
        if cond is None:
            desc.start()
        else:
            pl.when(cond)(desc.start)
        waits.append((cond, desc))

    my_i = lax.rem(b, per)
    for h in range(halves):
        src = z_ref.at[pl.ds(h * part, part)]
        r = recv_sem.at[index(my_i, p, h)]
        send_if(mine != p, remote(src, slot(my_i, p, h), x_sem.at[h], r, mine, b))

        @pl.when(mine == p)
        def _():
            pltpu.make_async_copy(src, slot(my_i, p, h), r).start()

    for d in range(1, blks):
        other = lax.rem(b + d, blks)
        send_if(None, remote(part_ref, pg.at[b], ps_sem.at[d], pr_sem.at[b], p, other))

    def w_copy(i):
        cols = pl.ds(pl.multiple_of(i * block, block), block)
        return pltpu.make_async_copy(w_hbm.at[:, cols], wbuf.at[i], w_sem.at[i])

    flip = z > first

    def source_of(g):
        return jnp.where(flip, srcs - 1 - g, g)

    for g in range(srcs):
        for j in range(group):
            w_copy(source_of(g) * group + j).start()
    acc[...] = jnp.zeros_like(acc)

    def arrive(i, pp, h):
        ref = slot(i, pp, h)
        k = index(i, pp, h)
        remote(ref, ref, x_sem.at[0], recv_sem.at[k], p, lax.rem(b + 1, blks)).wait_recv()

    def pass_on(i, pp, h, sem, cond, bb):
        k = index(i, pp, h)
        ref = slot(i, pp, h)
        send_if(cond, remote(ref, ref, sem, recv_sem.at[k], p, bb))

    def sibling():
        return (z * ys + y) * CORES + (1 - c)

    def line(g, pp, h):
        zs = source_of(g)
        i = zs * group + y * CORES + c
        k = index(i, pp, h)
        arrive(i, pp, h)
        origin = first + zs
        pass_on(i, pp, h, up_sem.at[k], (z >= origin) & (z < zs_all - 1), b + group)
        pass_on(i, pp, h, down_sem.at[k], (z <= origin) & (z > 0), b - group)
        for d in range(1, ys):
            other = (z * ys + lax.rem(y + d, ys)) * CORES + c
            pass_on(i, pp, h, y_sem.at[d, k], None, other)
        pass_on(i, pp, h, c_sem.at[k], None, sibling())

    def across(g, pp, h):
        for d in range(1, ys):
            i = source_of(g) * group + lax.rem(y + d, ys) * CORES + c
            arrive(i, pp, h)
            pass_on(i, pp, h, c_sem.at[index(i, pp, h)], None, sibling())

    def tile_dot(i, t):
        cols = pl.ds(t * wide if isinstance(t, int) else pl.multiple_of(t * wide, wide), wide)
        acc[:, cols] += lax.dot_general(
            gath[i], wbuf[i, cols, :], (((1,), (1,)), ((), ())),
            preferred_element_type=jnp.float32,
        )

    def other_core(g, yy):
        i = source_of(g) * group + yy * CORES + (1 - c)
        for q in range(pops):
            for h in range(halves):
                arrive(i, q, h)

    def ready(g):
        jobs = []
        for d in range(ys):
            yy = lax.rem(y + d, ys)
            jobs.append((source_of(g) * group + yy * CORES + c, None))
            jobs.append((source_of(g) * group + yy * CORES + (1 - c), yy))
        return [(g, i, yy) for i, yy in jobs]

    def multiply(job):
        g, i, yy = job
        if yy is not None:
            other_core(g, yy)
        w_copy(i).wait()

        @pl.loop(0, tiles)
        def _(t):
            tile_dot(i, t)

    steps = [(g, e, h) for g in range(srcs) for e in range(pops) for h in range(halves)]
    queue = []
    last = None
    for n, (g, e, h) in enumerate(steps):
        line(g, lax.rem(p + e, pops), h)
        if last is not None:
            across(last[0], lax.rem(p + last[1], pops), last[2])
            if last[0] != g:
                queue.extend(ready(last[0]))
        last = (g, e, h)
        if queue:
            multiply(queue.pop(0))
    for job in queue:
        multiply(job)
    final = ready(srcs - 1)
    multiply(final[0])
    across(last[0], lax.rem(p + last[1], pops), last[2])
    multiply(final[1])
    final = final[2:]
    for g, i, yy in final:
        if yy is not None:
            other_core(g, yy)
        w_copy(i).wait()
    for t in range(tiles):
        for g, i, yy in final:
            tile_dot(i, t)
        for d in range(1, pops):
            pp = lax.rem(p + d, pops)
            half = acc[pl.ds(pl.multiple_of(pp * rows, rows), rows), pl.ds(t * wide, wide)]
            sendp[t, d] = half.astype(sendp.dtype)
            send_if(None, remote(
                sendp.at[t, d], recvp.at[t, p], ss_sem.at[t, d], sr_sem.at[t, p], pp, b))

    pg[b] = part_ref[...]
    for d in range(1, blks):
        other = lax.rem(b + d, blks)
        remote(part_ref, pg.at[other], ps_sem.at[d], pr_sem.at[other], p, other).wait_recv()
    total = pg[0]
    for d in range(1, blks):
        total = total + pg[d]
    proj_ref[...] = total

    for t in range(tiles):
        cols = pl.ds(t * wide, wide)
        value = acc[pl.ds(pl.multiple_of(p * rows, rows), rows), cols]
        for d in range(1, pops):
            pp = lax.rem(p + d, pops)
            remote(
                sendp.at[t, d], recvp.at[t, pp], ss_sem.at[t, d], sr_sem.at[t, pp], pp, b
            ).wait_recv()
            value = value + recvp[t, pp].astype(jnp.float32)
        out_ref[:, cols] = value

    for cond, desc in waits:
        if cond is None:
            desc.wait_send()
        else:
            pl.when(cond)(desc.wait_send)


def exchange(pops, blks, spikes, part, weight):
    rows, block = spikes.shape
    outs = weight.shape[0]
    per = blks // pops
    ys, _ = factor_plane(blks)
    halves = 2
    tiles = max(1, outs // 256)
    slots = blks * halves
    dma = pltpu.SemaphoreType.DMA
    vmem = pl.BlockSpec(memory_space=pltpu.VMEM)
    flops = 2 * pops * rows * weight.size
    return pl.pallas_call(
        functools.partial(kernel, pops, blks, halves, tiles),
        out_shape=(
            jax.ShapeDtypeStruct((rows, outs), jnp.float32),
            jax.ShapeDtypeStruct(part.shape, jnp.float32),
        ),
        in_specs=[vmem, vmem, pl.BlockSpec(memory_space=pl.ANY)],
        out_specs=(vmem, vmem),
        scratch_shapes=[
            pltpu.VMEM((per, pops * rows, block), spikes.dtype),
            pltpu.VMEM((per, outs, block), weight.dtype),
            pltpu.VMEM((pops * rows, outs), jnp.float32),
            pltpu.VMEM((tiles, pops, rows, outs // tiles), jnp.bfloat16),
            pltpu.VMEM((tiles, pops, rows, outs // tiles), jnp.bfloat16),
            pltpu.VMEM((blks,) + part.shape, jnp.float32),
            dma((per,)),
            dma((slots,)),
            dma((halves,)),
            dma((slots,)),
            dma((slots,)),
            dma((ys, slots)),
            dma((slots,)),
            dma((blks,)),
            dma((blks,)),
            dma((tiles, pops)),
            dma((tiles, pops)),
        ],
        compiler_params=pltpu.CompilerParams(
            has_side_effects=True, vmem_limit_bytes=40 * 2**20
        ),
        cost_estimate=pl.CostEstimate(
            flops=flops, bytes_accessed=weight.size * 2, transcendentals=0
        ),
    )(spikes, part, weight)


def body(
    pops,
    blks,
    v_init,
    a_init,
    z_init,
    base_weight,
    factor_u,
    factor_v,
    in_weight,
    spikes_in,
    step_count,
    member_ids,
    decay_mem,
    decay_adapt,
    thr_base,
    thr_adapt,
):
    members, trials, block = v_init.shape
    rank = factor_v.shape[1]
    rows = members * trials
    sign = (1 - 2 * (member_ids % 2)).astype(jnp.float32)
    state_v, state_a, spikes = (v_init, a_init, z_init)
    pad = -members % 128
    for step in range(STEPS):
        spikes_f = spikes.astype(jnp.float32)
        part = jnp.einsum(
            "mtn,mkn->tkm", spikes, factor_v, preferred_element_type=jnp.float32
        ).reshape(trials * rank, members)
        part = jnp.pad(part, ((0, 0), (0, pad)))
        dense, total = exchange(pops, blks, spikes.reshape(rows, block), part, base_weight)
        dense = dense.reshape(members, trials, block)
        proj = total[:, :members].reshape(trials, rank, members).astype(jnp.bfloat16)
        low = jnp.einsum("tkm,mkn->mtn", proj, factor_u, preferred_element_type=jnp.float32)
        current = jnp.dot(
            spikes_in[step].astype(jnp.bfloat16), in_weight, preferred_element_type=jnp.float32
        )
        drive = dense + 0.5 * sign[:, None, None] * low + current[None]
        v_new = (
            decay_mem * state_v
            + (1.0 - decay_mem) * drive
            - spikes_f * (thr_base + thr_adapt * state_a)
        )
        a_new = decay_adapt * state_a + (1.0 - decay_adapt) * spikes_f
        active = (step_count > step)[:, :, None]
        state_v = jnp.where(active, v_new, state_v)
        state_a = jnp.where(active, a_new, state_a)
        if step + 1 < STEPS:
            spikes = jax.nn.sigmoid(3.0 * (state_v - thr_base - thr_adapt * state_a)).astype(
                jnp.bfloat16
            )
    return (state_v, state_a)


def solution(mesh):
    in_specs = (
        P("pop", None, "blk"),
        P("pop", None, "blk"),
        P("pop", None, "blk"),
        P("blk", "pop"),
        P("pop", None, "blk"),
        P("pop", None, "blk"),
        P(None, "blk"),
        P(),
        P("pop", None),
        P("pop"),
        P("blk"),
        P("blk"),
        P("blk"),
        P("blk"),
    )
    out_specs = (P("pop", None, "blk"), P("pop", None, "blk"))
    return jax.shard_map(
        functools.partial(body, mesh.shape["pop"], mesh.shape["blk"]),
        mesh=mesh, in_specs=in_specs, out_specs=out_specs, check_vma=False,
    )
```
